32 devices in a mesh: amp: 8 (over y, x, core), slab: 4 (over z).
Axes of the slice: x: 2, y: 2, z: 4, core: 2. Of those that a mesh axis runs over, the one named last changes fastest.
Arguments:
- v_slab: bfloat16 [131072, 1024], P('amp', 'slab'), may hold values from -0.25 to 0.25
- t_amp: bfloat16 [8, 800, 1024], P(None, 'amp', 'slab'), may hold values from -6 to 6
- ab_tile_irrep: int32 [1024], replicated, may hold values from 0 to 7, as said below
Outputs:
- residual: bfloat16 [131072, 800], P(('amp', 'slab'))
The draws below stay inside these ranges and needn't reach their ends.
Inputs may be any that keep to these rules, and one draw needn't show every extreme that they name: `ab_tile_irrep`: Non-decreasing, takes every value from 0 to 7; the 128 consecutive tiles of one index of amp hold at most two distinct values, and in every draw some indices hold two.
All inputs are finite; a program needn't handle non-finite values.
Results may differ from the reference program's by a relative error of at most 0.009.
Values may be sent and summed in bfloat16 or wider, within the bound.
A program may use at most 192 MiB of HBM per device.

```python
import jax
import jax.numpy as jnp
from jax import lax

NIRR = 8
IJH = 800
CDH = 1024
TB = 128
AB_DEV = 16384
AB = 131072
ABT = 1024
N_SLAB = 4


def draw_ab_tile_irrep(key, part):
    key = jax.random.fold_in(key, 11)
    first_key, second_key = jax.random.split(key)
    tiles_local = AB_DEV // TB
    amp_count = ABT // tiles_local
    chosen_devices = jax.random.permutation(first_key, amp_count)[:NIRR - 1]
    sorted_devices = jnp.sort(chosen_devices).astype(jnp.int32)
    offsets = jax.random.randint(second_key, (NIRR - 1,), 1, tiles_local).astype(jnp.int32)
    boundary = sorted_devices * tiles_local + offsets
    position = jnp.arange(ABT, dtype=jnp.int32)
    return jnp.sum((position[:, None] >= boundary[None, :]).astype(jnp.int32), axis=1).astype(jnp.int32)


def strengthened(array, rng, source, target, blocks, factor):
    owner, partner = [(jnp.arange(array.shape[axis_at]) // (array.shape[axis_at] // blocks)).reshape([-1 if axis == axis_at else 1 for axis in range(array.ndim)]) for axis_at in (source, target)]
    chosen = jax.random.permutation(rng, blocks)[partner]
    strong = (owner == chosen) | (owner == (partner + blocks // 2) % blocks)
    return jnp.where(strong, factor * array, array)


def steps_of(key, extent, cuts, smallest, top_value):
    factor_of = 1.0
    for axis_at, shards_of in cuts:
        draws = jax.random.uniform(jax.random.fold_in(jax.random.fold_in(key, 6), axis_at), (shards_of,), jnp.float32, smallest / len(cuts), top_value / len(cuts))
        factor_of = factor_of * jnp.repeat(jnp.exp(draws), extent[axis_at] // shards_of).reshape((-1,) + (1,) * (len(extent) - 1 - axis_at))
    return factor_of


def centred(rng, shape, deviation, limit, cuts=(), kind=jnp.bfloat16):
    drawn = jax.random.normal(rng, shape, jnp.float32) * deviation
    if len(cuts) > 0:
        drawn = steps_of(rng, shape, cuts, -0.22, 0.18) * drawn
    return jnp.clip(drawn, min=-limit, max=limit).astype(kind)


def heavy_noise(stream_key, shape, scale, limit, pieces, heavy, held_as=jnp.bfloat16):
    values = scale * jax.random.normal(stream_key, shape, jnp.float32)
    if pieces:
        values = values * steps_of(stream_key, shape, pieces, -0.22, 0.18)
    return jnp.clip(strengthened(values, jax.random.fold_in(stream_key, 3), *heavy), -limit, limit).astype(held_as)


def setup_inputs(seed: int = 0) -> dict:
    key_list = jax.random.split(jax.random.key(seed), 4)
    v_slab = heavy_noise(key_list[0], (AB, CDH), CDH ** -0.5, 0.25, ((0, 8), (1, 4)), (1, 0, 8, 2.0))
    t_amp = centred(key_list[1], (NIRR, IJH, CDH), 1.0, 6.0, ((1, 8), (2, 4)))
    ab_tile_irrep = draw_ab_tile_irrep(jax.random.fold_in(key_list[3], 71), 0)
    return dict(v_slab=v_slab, t_amp=t_amp, ab_tile_irrep=ab_tile_irrep)


def reference(v_slab, t_amp, ab_tile_irrep):
    cd_block = CDH // N_SLAB

    def one_tile(operands):
        v_rows, irrep_index = operands
        amp_block = lax.dynamic_index_in_dim(t_amp, irrep_index.astype(jnp.int32), 0, keepdims=False)
        left_side = v_rows.astype(jnp.float32).reshape(TB, N_SLAB, cd_block)
        right_side = amp_block.astype(jnp.float32).reshape(IJH, N_SLAB, cd_block)
        partial_value = jnp.einsum("ksc,jsc->skj", left_side, right_side)
        partial_value = lax.optimization_barrier(partial_value.astype(jnp.bfloat16))
        return jnp.sum(partial_value.astype(jnp.float32), axis=0).astype(jnp.bfloat16)

    tile_blocks = v_slab.reshape(ABT, TB, CDH)
    residual = lax.map(one_tile, (tile_blocks, ab_tile_irrep))
    return residual.reshape(AB, IJH)
```

```python
import functools

import jax
import jax.numpy as jnp
from jax import lax
from jax.experimental import pallas as pl
from jax.experimental.pallas import tpu as pltpu
from jax.sharding import PartitionSpec as P

TB = 128
CHUNKS = 8
EARLY = 2
MESH = pl.DeviceIdType.MESH


def ladder_kernel(
    irrep_ref, t_ref, v_ref, out_ref,
    by_slab, packed, by_amp, stacked, right, v_rows, out_tiles,
    local_sem, tz_send, tz_recv, ta_send, ta_recv, v_send, v_recv, out_sem,
):
    amp_n, slab_n = lax.axis_size("amp"), lax.axis_size("slab")
    amp, slab = lax.axis_index("amp"), lax.axis_index("slab")
    ij = t_ref.shape[1]
    cd = v_ref.shape[1]
    rows_out = out_ref.shape[0]
    chunk = rows_out // CHUNKS
    tiles = irrep_ref.shape[0] // amp_n

    barrier = pltpu.get_barrier_semaphore()

    def greet_slab(k, _):
        pl.semaphore_signal(barrier, inc=1, device_id=(amp, lax.rem(slab + k, slab_n)), device_id_type=MESH)
        return 0

    def greet_amp(k, _):
        pl.semaphore_signal(barrier, inc=1, device_id=(lax.rem(amp + k, amp_n), slab), device_id_type=MESH)
        return 0

    lax.fori_loop(1, slab_n, greet_slab, 0)
    lax.fori_loop(1, amp_n, greet_amp, 0)
    pl.semaphore_wait(barrier, slab_n + amp_n - 2)

    def slab_copy(k):
        return pltpu.make_async_remote_copy(
            src_ref=t_ref, dst_ref=by_slab.at[slab],
            send_sem=tz_send.at[k], recv_sem=tz_recv.at[k],
            device_id=(amp, lax.rem(slab + k, slab_n)), device_id_type=MESH,
        )

    def start_slab(k, _):
        slab_copy(k).start()
        return 0

    lax.fori_loop(1, slab_n, start_slab, 0)
    own_t = pltpu.make_async_copy(t_ref, by_slab.at[slab], local_sem.at[0])
    own_t.start()

    def v_copy(c, k):
        to = lax.rem(slab + k, slab_n)
        return pltpu.make_async_remote_copy(
            src_ref=v_ref.at[pl.ds(pl.multiple_of(to * rows_out + c * chunk, chunk), chunk)],
            dst_ref=v_rows.at[slab, pl.ds(pl.multiple_of(c * chunk, chunk), chunk)],
            send_sem=v_send.at[c, k], recv_sem=v_recv.at[c, k],
            device_id=(amp, to), device_id_type=MESH,
        )

    def start_v(c, _):
        def one(k, _):
            v_copy(c, k).start()
            return 0

        return lax.fori_loop(1, slab_n, one, 0)

    lax.fori_loop(0, EARLY, start_v, 0)
    own_v = pltpu.make_async_copy(
        v_ref.at[pl.ds(pl.multiple_of(slab * rows_out, chunk), rows_out)], v_rows.at[slab], local_sem.at[1]
    )
    own_v.start()

    own_t.wait()

    def await_slab(k, _):
        slab_copy(k).wait()
        return 0

    lax.fori_loop(1, slab_n, await_slab, 0)

    def amp_copy(k):
        return pltpu.make_async_remote_copy(
            src_ref=packed.at[k], dst_ref=by_amp.at[amp],
            send_sem=ta_send.at[k], recv_sem=ta_recv.at[k],
            device_id=(lax.rem(amp + k, amp_n), slab), device_id_type=MESH,
        )

    def pack(k, _):
        to = lax.rem(amp + k, amp_n)
        first, last = irrep_ref[to * tiles], irrep_ref[to * tiles + tiles - 1]

        def one(s, _):
            packed[k, 0, s] = by_slab[s, first]
            packed[k, 1, s] = by_slab[s, last]
            return 0

        lax.fori_loop(0, slab_n, one, 0)
        amp_copy(k).start()
        return 0

    lax.fori_loop(1, amp_n, pack, 0)
    lax.fori_loop(EARLY, CHUNKS, start_v, 0)
    first, last = irrep_ref[amp * tiles], irrep_ref[amp * tiles + tiles - 1]

    def keep(s, _):
        by_amp[amp, 0, s] = by_slab[s, first]
        by_amp[amp, 1, s] = by_slab[s, last]
        return 0

    lax.fori_loop(0, slab_n, keep, 0)
    stacked[...] = jnp.zeros_like(stacked)

    def await_amp(k, _):
        amp_copy(k).wait()
        return 0

    lax.fori_loop(1, amp_n, await_amp, 0)

    def assemble(step, _):
        b, s = step // slab_n, lax.rem(step, slab_n)
        for a in range(amp_n):
            stacked[a * ij:(a + 1) * ij, :] = by_amp[a, b, s].astype(jnp.float32)
        right[b, s] = stacked[...].T.astype(jnp.bfloat16)
        return 0

    lax.fori_loop(0, 2 * slab_n, assemble, 0)
    own_v.wait()

    def out_copy(c):
        place = lax.rem(c, 2)
        return pltpu.make_async_copy(
            out_tiles.at[place], out_ref.at[pl.ds(pl.multiple_of(c * chunk, chunk), chunk)], out_sem.at[place]
        )

    def multiply(c, _):
        def await_v(k, _):
            v_copy(c, k).wait_recv()
            return 0

        lax.fori_loop(1, slab_n, await_v, 0)

        @pl.when(c >= 2)
        def _():
            out_copy(c - 2).wait()

        def tile(i, _):
            at = slab * (rows_out // TB) + c * (chunk // TB) + i
            slot = (irrep_ref[amp * tiles + at] != first).astype(jnp.int32)
            total = jnp.zeros((TB, right.shape[3]), jnp.float32)
            for s in range(slab_n):
                rows = v_rows[s, pl.ds(pl.multiple_of(c * chunk + i * TB, TB), TB)]
                total += jnp.dot(rows, right[slot, s], preferred_element_type=jnp.float32)
            out_tiles[lax.rem(c, 2), pl.ds(pl.multiple_of(i * TB, TB), TB)] = (
                total[:, :out_tiles.shape[2]].astype(jnp.bfloat16)
            )
            return 0

        lax.fori_loop(0, chunk // TB, tile, 0)
        out_copy(c).start()
        return 0

    lax.fori_loop(0, CHUNKS, multiply, 0)
    out_copy(CHUNKS - 2).wait()
    out_copy(CHUNKS - 1).wait()

    def sent(c, _):
        def one(k, _):
            v_copy(c, k).wait_send()
            return 0

        return lax.fori_loop(1, slab_n, one, 0)

    lax.fori_loop(0, CHUNKS, sent, 0)


def on_device(v_slab, t_amp, ab_tile_irrep):
    rows_local, cd = v_slab.shape
    irreps, ij = t_amp.shape[:2]
    amp_n, slab_n = lax.axis_size("amp"), lax.axis_size("slab")
    rows_out = rows_local // slab_n
    ij_all = ij * amp_n
    wide = -(-ij_all // 128) * 128
    any_space = pl.BlockSpec(memory_space=pl.ANY)
    return pl.pallas_call(
        ladder_kernel,
        out_shape=jax.ShapeDtypeStruct((rows_out, ij_all), jnp.bfloat16),
        in_specs=[pl.BlockSpec(memory_space=pltpu.SMEM), any_space, any_space],
        out_specs=any_space,
        scratch_shapes=[
            pltpu.VMEM((slab_n, irreps, ij, cd), jnp.bfloat16),
            pltpu.VMEM((amp_n, 2, slab_n, ij, cd), jnp.bfloat16),
            pltpu.VMEM((amp_n, 2, slab_n, ij, cd), jnp.bfloat16),
            pltpu.VMEM((wide, cd), jnp.float32),
            pltpu.VMEM((2, slab_n, cd, wide), jnp.bfloat16),
            pltpu.VMEM((slab_n, rows_out, cd), jnp.bfloat16),
            pltpu.VMEM((2, rows_out // CHUNKS, ij_all), jnp.bfloat16),
            pltpu.SemaphoreType.DMA((2,)),
            pltpu.SemaphoreType.DMA((slab_n,)),
            pltpu.SemaphoreType.DMA((slab_n,)),
            pltpu.SemaphoreType.DMA((amp_n,)),
            pltpu.SemaphoreType.DMA((amp_n,)),
            pltpu.SemaphoreType.DMA((CHUNKS, slab_n)),
            pltpu.SemaphoreType.DMA((CHUNKS, slab_n)),
            pltpu.SemaphoreType.DMA((2,)),
        ],
        compiler_params=pltpu.CompilerParams(
            collective_id=0, has_side_effects=True, vmem_limit_bytes=48 * 1024 * 1024
        ),
        cost_estimate=pl.CostEstimate(
            flops=2 * rows_out * cd * slab_n * ij_all,
            bytes_accessed=2 * (rows_local * cd + rows_out * ij_all),
            transcendentals=0,
        ),
    )(ab_tile_irrep, t_amp, v_slab)


def solution(mesh):
    placed = (P("amp", "slab"), P(None, "amp", "slab"), P())
    return jax.shard_map(
        on_device, mesh=mesh, in_specs=placed, out_specs=P(("amp", "slab"), None), check_vma=False
    )
```

```python
import functools

import jax
import jax.numpy as jnp
from jax import lax
from jax.experimental import pallas as pl
from jax.experimental.pallas import tpu as pltpu
from jax.sharding import PartitionSpec as P

TB = 128
CHUNKS = 8
EARLY = 2
MESH = pl.DeviceIdType.MESH


def ladder_kernel(
    irreps_in, t_ref, v_ref, out_ref,
    irrep_ref, by_slab, packed, by_amp, stacked, left, v_rows, out_tiles,
    local_sem, tz_send, tz_recv, ta_send, ta_recv, v_send, v_recv, out_sem,
):
    amp_n, slab_n = lax.axis_size("amp"), lax.axis_size("slab")
    amp, slab = lax.axis_index("amp"), lax.axis_index("slab")
    ij = t_ref.shape[1]
    cd = v_ref.shape[1]
    rows_out = out_ref.shape[1]
    chunk = rows_out // CHUNKS
    tiles = irrep_ref.shape[0] // amp_n

    own_irreps = pltpu.make_async_copy(irreps_in, irrep_ref, local_sem.at[2])
    own_irreps.start()

    barrier = pltpu.get_barrier_semaphore()

    def greet_slab(k, _):
        pl.semaphore_signal(barrier, inc=1, device_id=(amp, lax.rem(slab + k, slab_n)), device_id_type=MESH)
        return 0

    def greet_amp(k, _):
        pl.semaphore_signal(barrier, inc=1, device_id=(lax.rem(amp + k, amp_n), slab), device_id_type=MESH)
        return 0

    lax.fori_loop(1, slab_n, greet_slab, 0)
    lax.fori_loop(1, amp_n, greet_amp, 0)
    pl.semaphore_wait(barrier, slab_n + amp_n - 2)

    def hop(way, r):
        source = slab - r if way == 0 else slab + r
        to = slab + 1 if way == 0 else slab - 1
        held = jnp.clip(source, 0, slab_n - 1)
        return pltpu.make_async_remote_copy(
            src_ref=t_ref if r == 0 else by_slab.at[held], dst_ref=by_slab.at[held],
            send_sem=tz_send.at[way, r], recv_sem=tz_recv.at[held],
            device_id=(amp, jnp.clip(to, 0, slab_n - 1)), device_id_type=MESH,
        )

    def has(way, r):
        return slab - r >= 0 if way == 0 else slab + r < slab_n

    def passes(way, r):
        return jnp.logical_and(has(way, r), slab + 1 < slab_n if way == 0 else slab > 0)

    for way in range(2):
        @pl.when(passes(way, 0))
        def _():
            hop(way, 0).start()

    own_t = pltpu.make_async_copy(t_ref, by_slab.at[slab], local_sem.at[0])
    own_t.start()

    def v_copy(c, k):
        to = lax.rem(slab + k, slab_n)
        return pltpu.make_async_remote_copy(
            src_ref=v_ref.at[pl.ds(pl.multiple_of(to * rows_out + c * chunk, chunk), chunk)],
            dst_ref=v_rows.at[slab, pl.ds(pl.multiple_of(c * chunk, chunk), chunk)],
            send_sem=v_send.at[c, k], recv_sem=v_recv.at[c, k],
            device_id=(amp, to), device_id_type=MESH,
        )

    def start_v(c, _):
        def one(k, _):
            v_copy(c, k).start()
            return 0

        return lax.fori_loop(1, slab_n, one, 0)

    lax.fori_loop(0, EARLY, start_v, 0)
    own_v = pltpu.make_async_copy(
        v_ref.at[pl.ds(pl.multiple_of(slab * rows_out, chunk), rows_out)], v_rows.at[slab], local_sem.at[1]
    )
    own_v.start()

    own_irreps.wait()
    own_t.wait()

    for r in range(1, slab_n):
        for way in range(2):
            @pl.when(has(way, r))
            def _():
                hop(way, r).wait_recv()

            if r < slab_n - 1:
                @pl.when(passes(way, r))
                def _():
                    hop(way, r).start()

    def amp_copy(k):
        return pltpu.make_async_remote_copy(
            src_ref=packed.at[k], dst_ref=by_amp.at[amp],
            send_sem=ta_send.at[k], recv_sem=ta_recv.at[k],
            device_id=(lax.rem(amp + k, amp_n), slab), device_id_type=MESH,
        )

    def pack(k, _):
        to = lax.rem(amp + k, amp_n)
        first, last = irrep_ref[to * tiles], irrep_ref[to * tiles + tiles - 1]

        def one(s, _):
            packed[k, 0, s] = by_slab[s, first]
            packed[k, 1, s] = by_slab[s, last]
            return 0

        lax.fori_loop(0, slab_n, one, 0)
        amp_copy(k).start()
        return 0

    lax.fori_loop(1, amp_n, pack, 0)
    lax.fori_loop(EARLY, CHUNKS, start_v, 0)
    first, last = irrep_ref[amp * tiles], irrep_ref[amp * tiles + tiles - 1]

    def keep(s, _):
        by_amp[amp, 0, s] = by_slab[s, first]
        by_amp[amp, 1, s] = by_slab[s, last]
        return 0

    lax.fori_loop(0, slab_n, keep, 0)

    def await_amp(k, _):
        amp_copy(k).wait()
        return 0

    lax.fori_loop(1, amp_n, await_amp, 0)

    def assemble(step, _):
        b, s = step // slab_n, lax.rem(step, slab_n)
        for a in range(amp_n):
            stacked[a * ij:(a + 1) * ij, :] = by_amp[a, b, s].astype(jnp.float32)
        left[b, s] = stacked[...].astype(jnp.bfloat16)
        return 0

    lax.fori_loop(0, 2 * slab_n, assemble, 0)
    own_v.wait()

    def out_copy(c):
        place = lax.rem(c, 2)
        return pltpu.make_async_copy(
            out_tiles.at[place], out_ref.at[:, pl.ds(pl.multiple_of(c * chunk, chunk), chunk)], out_sem.at[place]
        )

    def multiply(c, _):
        def await_v(k, _):
            v_copy(c, k).wait_recv()
            return 0

        lax.fori_loop(1, slab_n, await_v, 0)

        @pl.when(c >= 2)
        def _():
            out_copy(c - 2).wait()

        def tile(i, _):
            at = slab * (rows_out // TB) + c * (chunk // TB) + i
            slot = (irrep_ref[amp * tiles + at] != first).astype(jnp.int32)
            total = jnp.zeros((left.shape[2], TB), jnp.float32)
            for s in range(slab_n):
                rows = v_rows[s, pl.ds(pl.multiple_of(c * chunk + i * TB, TB), TB)]
                total += lax.dot_general(
                    left[slot, s], rows, (((1,), (1,)), ((), ())), preferred_element_type=jnp.float32
                )
            out_tiles[lax.rem(c, 2), :, pl.ds(pl.multiple_of(i * TB, TB), TB)] = total.astype(jnp.bfloat16)
            return 0

        lax.fori_loop(0, chunk // TB, tile, 0)
        out_copy(c).start()
        return 0

    lax.fori_loop(0, CHUNKS, multiply, 0)
    out_copy(CHUNKS - 2).wait()
    out_copy(CHUNKS - 1).wait()

    def sent(c, _):
        def one(k, _):
            v_copy(c, k).wait_send()
            return 0

        return lax.fori_loop(1, slab_n, one, 0)

    lax.fori_loop(0, CHUNKS, sent, 0)
    for r in range(slab_n - 1):
        for way in range(2):
            @pl.when(passes(way, r))
            def _():
                hop(way, r).wait_send()


def on_device(v_slab, t_amp, ab_tile_irrep):
    rows_local, cd = v_slab.shape
    irreps, ij = t_amp.shape[:2]
    amp_n, slab_n = lax.axis_size("amp"), lax.axis_size("slab")
    rows_out = rows_local // slab_n
    ij_all = ij * amp_n
    any_space = pl.BlockSpec(memory_space=pl.ANY)
    return pl.pallas_call(
        ladder_kernel,
        out_shape=jax.ShapeDtypeStruct((ij_all, rows_out), jnp.bfloat16),
        in_specs=[any_space] * 3,
        out_specs=any_space,
        scratch_shapes=[
            pltpu.SMEM(ab_tile_irrep.shape, jnp.int32),
            pltpu.VMEM((slab_n, irreps, ij, cd), jnp.bfloat16),
            pltpu.VMEM((amp_n, 2, slab_n, ij, cd), jnp.bfloat16),
            pltpu.VMEM((amp_n, 2, slab_n, ij, cd), jnp.bfloat16),
            pltpu.VMEM((ij_all, cd), jnp.float32),
            pltpu.VMEM((2, slab_n, ij_all, cd), jnp.bfloat16),
            pltpu.VMEM((slab_n, rows_out, cd), jnp.bfloat16),
            pltpu.VMEM((2, ij_all, rows_out // CHUNKS), jnp.bfloat16),
            pltpu.SemaphoreType.DMA((3,)),
            pltpu.SemaphoreType.DMA((2, slab_n)),
            pltpu.SemaphoreType.DMA((slab_n,)),
            pltpu.SemaphoreType.DMA((amp_n,)),
            pltpu.SemaphoreType.DMA((amp_n,)),
            pltpu.SemaphoreType.DMA((CHUNKS, slab_n)),
            pltpu.SemaphoreType.DMA((CHUNKS, slab_n)),
            pltpu.SemaphoreType.DMA((2,)),
        ],
        compiler_params=pltpu.CompilerParams(
            collective_id=0, has_side_effects=True, vmem_limit_bytes=48 * 1024 * 1024
        ),
        cost_estimate=pl.CostEstimate(
            flops=2 * rows_out * cd * slab_n * ij_all,
            bytes_accessed=2 * (rows_local * cd + rows_out * ij_all),
            transcendentals=0,
        ),
    )(ab_tile_irrep, t_amp, v_slab).T


def solution(mesh):
    placed = (P("amp", "slab"), P(None, "amp", "slab"), P())
    return jax.shard_map(
        on_device, mesh=mesh, in_specs=placed, out_specs=P(("amp", "slab"), None), check_vma=False
    )
```

```python
import functools

import jax
import jax.numpy as jnp
from jax import lax
from jax.experimental import pallas as pl
from jax.experimental.pallas import tpu as pltpu
from jax.sharding import PartitionSpec as P

TB = 128
LANES = 128
CHUNKS = 8
EARLY = 2
MESH = pl.DeviceIdType.MESH


def ladder_kernel(
    irreps_in, t_ref, v_ref, out_ref,
    irrep_ref, by_slab, spread, packed, by_amp, stacked, left, v_rows,
    local_sem, tz_send, tz_recv, ta_send, ta_recv, v_send, v_recv,
):
    amp_n, slab_n = lax.axis_size("amp"), lax.axis_size("slab")
    amp, slab = lax.axis_index("amp"), lax.axis_index("slab")
    ij, irreps = t_ref.shape[:2]
    cd = v_ref.shape[1]
    rows_out = out_ref.shape[1]
    chunk = rows_out // CHUNKS
    tiles = irrep_ref.shape[0] // amp_n

    own_irreps = pltpu.make_async_copy(irreps_in, irrep_ref, local_sem.at[2])
    own_irreps.start()

    barrier = pltpu.get_barrier_semaphore()

    def greet_slab(k, _):
        pl.semaphore_signal(barrier, inc=1, device_id=(amp, lax.rem(slab + k, slab_n)), device_id_type=MESH)
        return 0

    def greet_amp(k, _):
        pl.semaphore_signal(barrier, inc=1, device_id=(lax.rem(amp + k, amp_n), slab), device_id_type=MESH)
        return 0

    lax.fori_loop(1, slab_n, greet_slab, 0)
    lax.fori_loop(1, amp_n, greet_amp, 0)
    pl.semaphore_wait(barrier, slab_n + amp_n - 2)

    def hop(way, r):
        source = slab - r if way == 0 else slab + r
        to = slab + 1 if way == 0 else slab - 1
        held = jnp.clip(source, 0, slab_n - 1)
        return pltpu.make_async_remote_copy(
            src_ref=t_ref if r == 0 else by_slab.at[held], dst_ref=by_slab.at[held],
            send_sem=tz_send.at[way, r], recv_sem=tz_recv.at[held],
            device_id=(amp, jnp.clip(to, 0, slab_n - 1)), device_id_type=MESH,
        )

    def has(way, r):
        return slab - r >= 0 if way == 0 else slab + r < slab_n

    def passes(way, r):
        return jnp.logical_and(has(way, r), slab + 1 < slab_n if way == 0 else slab > 0)

    for way in range(2):
        @pl.when(passes(way, 0))
        def _():
            hop(way, 0).start()

    own_t = pltpu.make_async_copy(t_ref, by_slab.at[slab], local_sem.at[0])
    own_t.start()

    def v_copy(c, k):
        to = lax.rem(slab + k, slab_n)
        return pltpu.make_async_remote_copy(
            src_ref=v_ref.at[pl.ds(pl.multiple_of(to * rows_out + c * chunk, chunk), chunk)],
            dst_ref=v_rows.at[slab, pl.ds(pl.multiple_of(c * chunk, chunk), chunk)],
            send_sem=v_send.at[c, k], recv_sem=v_recv.at[c, k],
            device_id=(amp, to), device_id_type=MESH,
        )

    def start_v(c, _):
        def one(k, _):
            v_copy(c, k).start()
            return 0

        return lax.fori_loop(1, slab_n, one, 0)

    lax.fori_loop(0, EARLY, start_v, 0)
    own_v = pltpu.make_async_copy(
        v_ref.at[pl.ds(pl.multiple_of(slab * rows_out, chunk), rows_out)], v_rows.at[slab], local_sem.at[1]
    )
    own_v.start()

    own_irreps.wait()
    own_t.wait()

    for r in range(1, slab_n):
        for way in range(2):
            @pl.when(has(way, r))
            def _():
                hop(way, r).wait_recv()

            if r < slab_n - 1:
                @pl.when(passes(way, r))
                def _():
                    hop(way, r).start()

    def amp_copy(k):
        return pltpu.make_async_remote_copy(
            src_ref=packed.at[k], dst_ref=by_amp.at[amp],
            send_sem=ta_send.at[k], recv_sem=ta_recv.at[k],
            device_id=(lax.rem(amp + k, amp_n), slab), device_id_type=MESH,
        )

    def widen(s, _):
        whole = by_slab[s].astype(jnp.float32).reshape(ij * irreps, cd)
        for q in range(cd // LANES):
            spread[s, q] = whole[:, q * LANES:(q + 1) * LANES]
        return 0

    lax.fori_loop(0, slab_n, widen, 0)

    def block_of(s, irrep):
        parts = [spread[s, q, pl.ds(irrep, ij, irreps), :] for q in range(cd // LANES)]
        return jnp.concatenate(parts, axis=1).astype(jnp.bfloat16)

    def pack(k, _):
        to = lax.rem(amp + k, amp_n)
        first, last = irrep_ref[to * tiles], irrep_ref[to * tiles + tiles - 1]

        def one(s, _):
            packed[k, 0, s] = block_of(s, first)
            packed[k, 1, s] = block_of(s, last)
            return 0

        lax.fori_loop(0, slab_n, one, 0)
        amp_copy(k).start()
        return 0

    lax.fori_loop(1, amp_n, pack, 0)
    lax.fori_loop(EARLY, CHUNKS, start_v, 0)
    first, last = irrep_ref[amp * tiles], irrep_ref[amp * tiles + tiles - 1]

    def keep(s, _):
        by_amp[amp, 0, s] = block_of(s, first)
        by_amp[amp, 1, s] = block_of(s, last)
        return 0

    lax.fori_loop(0, slab_n, keep, 0)

    def await_amp(k, _):
        amp_copy(k).wait()
        return 0

    lax.fori_loop(1, amp_n, await_amp, 0)

    def assemble(step, _):
        b, s = step // slab_n, lax.rem(step, slab_n)
        for a in range(amp_n):
            stacked[a * ij:(a + 1) * ij, :] = by_amp[a, b, s].astype(jnp.float32)
        left[b, s] = stacked[...].astype(jnp.bfloat16)
        return 0

    lax.fori_loop(0, 2 * slab_n, assemble, 0)
    own_v.wait()

    def multiply(c, _):
        def await_v(k, _):
            v_copy(c, k).wait_recv()
            return 0

        lax.fori_loop(1, slab_n, await_v, 0)

        def tile(i, _):
            at = slab * (rows_out // TB) + c * (chunk // TB) + i
            slot = (irrep_ref[amp * tiles + at] != first).astype(jnp.int32)
            total = jnp.zeros((left.shape[2], TB), jnp.float32)
            for s in range(slab_n):
                rows = v_rows[s, pl.ds(pl.multiple_of(c * chunk + i * TB, TB), TB)]
                total += lax.dot_general(
                    left[slot, s], rows, (((1,), (1,)), ((), ())), preferred_element_type=jnp.float32
                )
            out_ref[:, pl.ds(pl.multiple_of(c * chunk + i * TB, TB), TB)] = total.astype(jnp.bfloat16)
            return 0

        lax.fori_loop(0, chunk // TB, tile, 0)
        return 0

    lax.fori_loop(0, CHUNKS, multiply, 0)

    def sent(c, _):
        def one(k, _):
            v_copy(c, k).wait_send()
            return 0

        return lax.fori_loop(1, slab_n, one, 0)

    lax.fori_loop(0, CHUNKS, sent, 0)
    for r in range(slab_n - 1):
        for way in range(2):
            @pl.when(passes(way, r))
            def _():
                hop(way, r).wait_send()


def on_device(v_slab, t_amp, ab_tile_irrep):
    rows_local, cd = v_slab.shape
    irreps, ij = t_amp.shape[:2]
    amp_n, slab_n = lax.axis_size("amp"), lax.axis_size("slab")
    rows_out = rows_local // slab_n
    ij_all = ij * amp_n
    hbm = pl.BlockSpec(memory_space=pltpu.HBM)
    return pl.pallas_call(
        ladder_kernel,
        out_shape=jax.ShapeDtypeStruct((ij_all, rows_out), jnp.bfloat16),
        in_specs=[hbm] * 3,
        out_specs=pl.BlockSpec(memory_space=pltpu.VMEM),
        scratch_shapes=[
            pltpu.SMEM(ab_tile_irrep.shape, jnp.int32),
            pltpu.VMEM((slab_n, ij, irreps, cd), jnp.bfloat16),
            pltpu.VMEM((slab_n, cd // LANES, ij * irreps, LANES), jnp.float32),
            pltpu.VMEM((amp_n, 2, slab_n, ij, cd), jnp.bfloat16),
            pltpu.VMEM((amp_n, 2, slab_n, ij, cd), jnp.bfloat16),
            pltpu.VMEM((ij_all, cd), jnp.float32),
            pltpu.VMEM((2, slab_n, ij_all, cd), jnp.bfloat16),
            pltpu.VMEM((slab_n, rows_out, cd), jnp.bfloat16),
            pltpu.SemaphoreType.DMA((3,)),
            pltpu.SemaphoreType.DMA((2, slab_n)),
            pltpu.SemaphoreType.DMA((slab_n,)),
            pltpu.SemaphoreType.DMA((amp_n,)),
            pltpu.SemaphoreType.DMA((amp_n,)),
            pltpu.SemaphoreType.DMA((CHUNKS, slab_n)),
            pltpu.SemaphoreType.DMA((CHUNKS, slab_n)),
        ],
        compiler_params=pltpu.CompilerParams(
            collective_id=0, has_side_effects=True, vmem_limit_bytes=40 * 1024 * 1024
        ),
        cost_estimate=pl.CostEstimate(
            flops=2 * rows_out * cd * slab_n * ij_all,
            bytes_accessed=2 * (rows_local * cd + rows_out * ij_all),
            transcendentals=0,
        ),
    )(*[pltpu.with_memory_space_constraint(x, pltpu.HBM) for x in (ab_tile_irrep, t_amp.transpose(1, 0, 2), v_slab)]).T


def solution(mesh):
    placed = (P("amp", "slab"), P(None, "amp", "slab"), P())
    return jax.shard_map(
        on_device, mesh=mesh, in_specs=placed, out_specs=P(("amp", "slab"), None), check_vma=False
    )
```

```python
import functools

import jax
import jax.numpy as jnp
from jax import lax
from jax.experimental import pallas as pl
from jax.experimental.pallas import tpu as pltpu
from jax.sharding import PartitionSpec as P

TB = 128
LANES = 128
CHUNKS = 8
EARLY = 2
MESH = pl.DeviceIdType.MESH


def ladder_kernel(
    irreps_in, t_ref, v_ref, out_ref,
    irrep_ref, by_slab, spread, packed, by_amp, stacked, left, v_rows,
    local_sem, tz_send, tz_recv, ta_send, ta_recv, v_send, v_recv,
):
    amp_n, slab_n = lax.axis_size("amp"), lax.axis_size("slab")
    amp, slab = lax.axis_index("amp"), lax.axis_index("slab")
    ij, irreps = t_ref.shape[:2]
    cd = v_ref.shape[1]
    rows_out = out_ref.shape[1]
    chunk = rows_out // CHUNKS
    tiles = irrep_ref.shape[0] // amp_n

    own_irreps = pltpu.make_async_copy(irreps_in, irrep_ref, local_sem.at[2])
    own_irreps.start()

    barrier = pltpu.get_barrier_semaphore()

    def greet_slab(k, _):
        pl.semaphore_signal(barrier, inc=1, device_id=(amp, lax.rem(slab + k, slab_n)), device_id_type=MESH)
        return 0

    def greet_amp(k, _):
        pl.semaphore_signal(barrier, inc=1, device_id=(lax.rem(amp + k, amp_n), slab), device_id_type=MESH)
        return 0

    lax.fori_loop(1, slab_n, greet_slab, 0)
    lax.fori_loop(1, amp_n, greet_amp, 0)
    pl.semaphore_wait(barrier, slab_n + amp_n - 2)

    half = slab_n // 2
    low = slab < half
    near_first, far_first = jnp.where(low, 0, half), jnp.where(low, half, 0)
    far_gate = jnp.where(low, half, half - 1)
    at_gate = slab == jnp.where(low, half - 1, half)

    def own_copy(to):
        return pltpu.make_async_remote_copy(
            src_ref=t_ref, dst_ref=by_slab.at[slab], send_sem=tz_send.at[slab, to], recv_sem=tz_recv.at[slab],
            device_id=(amp, to), device_id_type=MESH,
        )

    def far_copy(source, to):
        return pltpu.make_async_remote_copy(
            src_ref=by_slab.at[source], dst_ref=by_slab.at[source],
            send_sem=tz_send.at[source, to], recv_sem=tz_recv.at[source],
            device_id=(amp, to), device_id_type=MESH,
        )

    own_copy(far_gate).start()
    for i in range(half):
        @pl.when(near_first + i != slab)
        def _():
            own_copy(near_first + i).start()

    own_t = pltpu.make_async_copy(t_ref, by_slab.at[slab], local_sem.at[0])
    own_t.start()

    def v_copy(c, k):
        to = lax.rem(slab + k, slab_n)
        return pltpu.make_async_remote_copy(
            src_ref=v_ref.at[pl.ds(pl.multiple_of(to * rows_out + c * chunk, chunk), chunk)],
            dst_ref=v_rows.at[slab, pl.ds(pl.multiple_of(c * chunk, chunk), chunk)],
            send_sem=v_send.at[c, k], recv_sem=v_recv.at[c, k],
            device_id=(amp, to), device_id_type=MESH,
        )

    def start_v(c, _):
        def one(k, _):
            v_copy(c, k).start()
            return 0

        return lax.fori_loop(1, slab_n, one, 0)

    lax.fori_loop(0, EARLY, start_v, 0)
    own_v = pltpu.make_async_copy(
        v_ref.at[pl.ds(pl.multiple_of(slab * rows_out, chunk), rows_out)], v_rows.at[slab], local_sem.at[1]
    )
    own_v.start()

    own_irreps.wait()
    own_t.wait()

    for i in range(half):
        far_copy(far_first + i, far_gate).wait_recv()
        for j in range(half):
            @pl.when(jnp.logical_and(at_gate, near_first + j != slab))
            def _():
                far_copy(far_first + i, near_first + j).start()

    for i in range(half):
        @pl.when(near_first + i != slab)
        def _():
            far_copy(near_first + i, far_gate).wait_recv()

    def amp_copy(k):
        return pltpu.make_async_remote_copy(
            src_ref=packed.at[k], dst_ref=by_amp.at[amp],
            send_sem=ta_send.at[k], recv_sem=ta_recv.at[k],
            device_id=(lax.rem(amp + k, amp_n), slab), device_id_type=MESH,
        )

    def widen(s, _):
        whole = by_slab[s].astype(jnp.float32).reshape(ij * irreps, cd)
        for q in range(cd // LANES):
            spread[s, q] = whole[:, q * LANES:(q + 1) * LANES]
        return 0

    lax.fori_loop(0, slab_n, widen, 0)

    def block_of(s, irrep):
        parts = [spread[s, q, pl.ds(irrep, ij, irreps), :] for q in range(cd // LANES)]
        return jnp.concatenate(parts, axis=1).astype(jnp.bfloat16)

    def pack(k, _):
        to = lax.rem(amp + k, amp_n)
        first, last = irrep_ref[to * tiles], irrep_ref[to * tiles + tiles - 1]

        def one(s, _):
            packed[k, 0, s] = block_of(s, first)
            packed[k, 1, s] = block_of(s, last)
            return 0

        lax.fori_loop(0, slab_n, one, 0)
        amp_copy(k).start()
        return 0

    lax.fori_loop(1, amp_n, pack, 0)
    lax.fori_loop(EARLY, CHUNKS, start_v, 0)
    first, last = irrep_ref[amp * tiles], irrep_ref[amp * tiles + tiles - 1]

    def keep(s, _):
        by_amp[amp, 0, s] = block_of(s, first)
        by_amp[amp, 1, s] = block_of(s, last)
        return 0

    lax.fori_loop(0, slab_n, keep, 0)

    def await_amp(k, _):
        amp_copy(k).wait()
        return 0

    lax.fori_loop(1, amp_n, await_amp, 0)

    def assemble(step, _):
        b, s = step // slab_n, lax.rem(step, slab_n)
        for a in range(amp_n):
            stacked[a * ij:(a + 1) * ij, :] = by_amp[a, b, s].astype(jnp.float32)
        left[b, s] = stacked[...].astype(jnp.bfloat16)
        return 0

    lax.fori_loop(0, 2 * slab_n, assemble, 0)
    own_v.wait()

    def multiply(c, _):
        def await_v(k, _):
            v_copy(c, k).wait_recv()
            return 0

        lax.fori_loop(1, slab_n, await_v, 0)

        def tile(i, _):
            at = slab * (rows_out // TB) + c * (chunk // TB) + i
            slot = (irrep_ref[amp * tiles + at] != first).astype(jnp.int32)
            total = jnp.zeros((left.shape[2], TB), jnp.float32)
            for s in range(slab_n):
                rows = v_rows[s, pl.ds(pl.multiple_of(c * chunk + i * TB, TB), TB)]
                total += lax.dot_general(
                    left[slot, s], rows, (((1,), (1,)), ((), ())), preferred_element_type=jnp.float32
                )
            out_ref[:, pl.ds(pl.multiple_of(c * chunk + i * TB, TB), TB)] = total.astype(jnp.bfloat16)
            return 0

        lax.fori_loop(0, chunk // TB, tile, 0)
        return 0

    lax.fori_loop(0, CHUNKS, multiply, 0)

    def sent(c, _):
        def one(k, _):
            v_copy(c, k).wait_send()
            return 0

        return lax.fori_loop(1, slab_n, one, 0)

    lax.fori_loop(0, CHUNKS, sent, 0)
    own_copy(far_gate).wait_send()
    for i in range(half):
        @pl.when(near_first + i != slab)
        def _():
            own_copy(near_first + i).wait_send()

        for j in range(half):
            @pl.when(jnp.logical_and(at_gate, near_first + j != slab))
            def _():
                far_copy(far_first + i, near_first + j).wait_send()


def on_device(v_slab, t_amp, ab_tile_irrep):
    rows_local, cd = v_slab.shape
    irreps, ij = t_amp.shape[:2]
    amp_n, slab_n = lax.axis_size("amp"), lax.axis_size("slab")
    rows_out = rows_local // slab_n
    ij_all = ij * amp_n
    hbm = pl.BlockSpec(memory_space=pltpu.HBM)
    return pl.pallas_call(
        ladder_kernel,
        out_shape=jax.ShapeDtypeStruct((ij_all, rows_out), jnp.bfloat16),
        in_specs=[hbm] * 3,
        out_specs=pl.BlockSpec(memory_space=pltpu.VMEM),
        scratch_shapes=[
            pltpu.SMEM(ab_tile_irrep.shape, jnp.int32),
            pltpu.VMEM((slab_n, ij, irreps, cd), jnp.bfloat16),
            pltpu.VMEM((slab_n, cd // LANES, ij * irreps, LANES), jnp.float32),
            pltpu.VMEM((amp_n, 2, slab_n, ij, cd), jnp.bfloat16),
            pltpu.VMEM((amp_n, 2, slab_n, ij, cd), jnp.bfloat16),
            pltpu.VMEM((ij_all, cd), jnp.float32),
            pltpu.VMEM((2, slab_n, ij_all, cd), jnp.bfloat16),
            pltpu.VMEM((slab_n, rows_out, cd), jnp.bfloat16),
            pltpu.SemaphoreType.DMA((3,)),
            pltpu.SemaphoreType.DMA((slab_n, slab_n)),
            pltpu.SemaphoreType.DMA((slab_n,)),
            pltpu.SemaphoreType.DMA((amp_n,)),
            pltpu.SemaphoreType.DMA((amp_n,)),
            pltpu.SemaphoreType.DMA((CHUNKS, slab_n)),
            pltpu.SemaphoreType.DMA((CHUNKS, slab_n)),
        ],
        compiler_params=pltpu.CompilerParams(
            collective_id=0, has_side_effects=True, vmem_limit_bytes=40 * 1024 * 1024
        ),
        cost_estimate=pl.CostEstimate(
            flops=2 * rows_out * cd * slab_n * ij_all,
            bytes_accessed=2 * (rows_local * cd + rows_out * ij_all),
            transcendentals=0,
        ),
    )(*[pltpu.with_memory_space_constraint(x, pltpu.HBM) for x in (ab_tile_irrep, t_amp.transpose(1, 0, 2), v_slab)]).T


def solution(mesh):
    placed = (P("amp", "slab"), P(None, "amp", "slab"), P())
    return jax.shard_map(
        on_device, mesh=mesh, in_specs=placed, out_specs=P(("amp", "slab"), None), check_vma=False
    )
```

```python
import functools

import jax
import jax.numpy as jnp
from jax import lax
from jax.experimental import pallas as pl
from jax.experimental.pallas import tpu as pltpu
from jax.sharding import PartitionSpec as P

TB = 128
LANES = 128
CHUNK = 4 * TB
EARLY = 2
AHEAD = 2
MESH = pl.DeviceIdType.MESH


def ladder_kernel(
    irreps_in, t_ref, v_ref, out_ref,
    irrep_ref, by_slab, spread, packed, by_amp, stacked, left, v_rows,
    local_sem, tz_send, tz_recv, ta_send, ta_recv, v_send, v_recv,
):
    amp_n, slab_n = lax.axis_size("amp"), lax.axis_size("slab")
    amp, slab = lax.axis_index("amp"), lax.axis_index("slab")
    ij, irreps = t_ref.shape[:2]
    cd = v_ref.shape[1]
    rows_out = out_ref.shape[1]
    long_n = rows_out // CHUNK - 1
    short_n = CHUNK // TB
    chunks = long_n + short_n
    tiles = irrep_ref.shape[0] // amp_n

    own_irreps = pltpu.make_async_copy(irreps_in, irrep_ref, local_sem.at[2])
    own_irreps.start()

    barrier = pltpu.get_barrier_semaphore()

    def greet_slab(k, _):
        pl.semaphore_signal(barrier, inc=1, device_id=(amp, lax.rem(slab + k, slab_n)), device_id_type=MESH)
        return 0

    def greet_amp(k, _):
        pl.semaphore_signal(barrier, inc=1, device_id=(lax.rem(amp + k, amp_n), slab), device_id_type=MESH)
        return 0

    lax.fori_loop(1, slab_n, greet_slab, 0)
    lax.fori_loop(1, amp_n, greet_amp, 0)
    pl.semaphore_wait(barrier, slab_n + amp_n - 2)

    half = slab_n // 2
    low = slab < half
    near_first, far_first = jnp.where(low, 0, half), jnp.where(low, half, 0)
    far_gate = jnp.where(low, half, half - 1)
    at_gate = slab == jnp.where(low, half - 1, half)

    def own_copy(to):
        return pltpu.make_async_remote_copy(
            src_ref=t_ref, dst_ref=by_slab.at[slab], send_sem=tz_send.at[slab, to], recv_sem=tz_recv.at[slab],
            device_id=(amp, to), device_id_type=MESH,
        )

    def far_copy(source, to):
        return pltpu.make_async_remote_copy(
            src_ref=by_slab.at[source], dst_ref=by_slab.at[source],
            send_sem=tz_send.at[source, to], recv_sem=tz_recv.at[source],
            device_id=(amp, to), device_id_type=MESH,
        )

    own_copy(far_gate).start()
    for i in range(half):
        @pl.when(near_first + i != slab)
        def _():
            own_copy(near_first + i).start()

    own_t = pltpu.make_async_copy(t_ref, by_slab.at[slab], local_sem.at[0])
    own_t.start()

    def place(c, size):
        if size == CHUNK:
            return pl.multiple_of(c * CHUNK, CHUNK)
        return pl.multiple_of(long_n * CHUNK + (c - long_n) * TB, TB)

    def v_copy(c, k, size):
        to = lax.rem(slab + k, slab_n)
        row = place(c, size)
        return pltpu.make_async_remote_copy(
            src_ref=v_ref.at[pl.ds(pl.multiple_of(to * rows_out + row, TB), size)],
            dst_ref=v_rows.at[slab, pl.ds(row, size)],
            send_sem=v_send.at[c, k], recv_sem=v_recv.at[c, k],
            device_id=(amp, to), device_id_type=MESH,
        )

    def start_v(size):
        def start(c, _):
            def one(k, _):
                v_copy(c, k, size).start()
                return 0

            return lax.fori_loop(1, slab_n, one, 0)

        return start

    early = min(EARLY, long_n)
    lax.fori_loop(0, early, start_v(CHUNK), 0)
    own_v = pltpu.make_async_copy(
        v_ref.at[pl.ds(pl.multiple_of(slab * rows_out, TB), rows_out)], v_rows.at[slab], local_sem.at[1]
    )
    own_v.start()

    own_irreps.wait()
    own_t.wait()

    for i in range(half):
        far_copy(far_first + i, far_gate).wait_recv()
        for j in range(half):
            @pl.when(jnp.logical_and(at_gate, near_first + j != slab))
            def _():
                far_copy(far_first + i, near_first + j).start()

    for i in range(half):
        @pl.when(near_first + i != slab)
        def _():
            far_copy(near_first + i, far_gate).wait_recv()

    def amp_copy(k):
        return pltpu.make_async_remote_copy(
            src_ref=packed.at[k], dst_ref=by_amp.at[amp],
            send_sem=ta_send.at[k], recv_sem=ta_recv.at[k],
            device_id=(lax.rem(amp + k, amp_n), slab), device_id_type=MESH,
        )

    def widen(s, _):
        whole = by_slab[s].astype(jnp.float32).reshape(ij * irreps, cd)
        for q in range(cd // LANES):
            spread[s, q] = whole[:, q * LANES:(q + 1) * LANES]
        return 0

    lax.fori_loop(0, slab_n, widen, 0)

    def block_of(s, irrep):
        parts = [spread[s, q, pl.ds(irrep, ij, irreps), :] for q in range(cd // LANES)]
        return jnp.concatenate(parts, axis=1).astype(jnp.bfloat16)

    def pack(k, _):
        to = lax.rem(amp + k, amp_n)
        first, last = irrep_ref[to * tiles], irrep_ref[to * tiles + tiles - 1]

        def one(s, _):
            packed[k, 0, s] = block_of(s, first)
            packed[k, 1, s] = block_of(s, last)
            return 0

        lax.fori_loop(0, slab_n, one, 0)
        amp_copy(k).start()
        return 0

    lax.fori_loop(1, amp_n, pack, 0)
    lax.fori_loop(early, long_n, start_v(CHUNK), 0)
    lax.fori_loop(long_n, long_n + AHEAD, start_v(TB), 0)
    first, last = irrep_ref[amp * tiles], irrep_ref[amp * tiles + tiles - 1]

    def keep(s, _):
        by_amp[amp, 0, s] = block_of(s, first)
        by_amp[amp, 1, s] = block_of(s, last)
        return 0

    lax.fori_loop(0, slab_n, keep, 0)

    def await_amp(k, _):
        amp_copy(k).wait()
        return 0

    lax.fori_loop(1, amp_n, await_amp, 0)

    def assemble(step, _):
        b, s = step // slab_n, lax.rem(step, slab_n)
        for a in range(amp_n):
            stacked[a * ij:(a + 1) * ij, :] = by_amp[a, b, s].astype(jnp.float32)
        left[b, s] = stacked[...].astype(jnp.bfloat16)
        return 0

    lax.fori_loop(0, 2 * slab_n, assemble, 0)
    own_v.wait()

    def multiply(size):
        def step(c, _):
            def await_v(k, _):
                v_copy(c, k, size).wait_recv()
                return 0

            lax.fori_loop(1, slab_n, await_v, 0)
            if size == TB:
                @pl.when(c + AHEAD < chunks)
                def _():
                    start_v(TB)(c + AHEAD, 0)

            row = place(c, size)

            def tile(i, _):
                at = pl.multiple_of(row + i * TB, TB)
                held = amp * tiles + slab * (rows_out // TB) + at // TB
                slot = (irrep_ref[held] != first).astype(jnp.int32)
                total = jnp.zeros((left.shape[2], TB), jnp.float32)
                for s in range(slab_n):
                    total += lax.dot_general(
                        left[slot, s], v_rows[s, pl.ds(at, TB)], (((1,), (1,)), ((), ())),
                        preferred_element_type=jnp.float32,
                    )
                out_ref[:, pl.ds(at, TB)] = total.astype(jnp.bfloat16)
                return 0

            return lax.fori_loop(0, size // TB, tile, 0)

        return step

    lax.fori_loop(0, long_n, multiply(CHUNK), 0)
    lax.fori_loop(long_n, chunks, multiply(TB), 0)

    def sent(size):
        def step(c, _):
            def one(k, _):
                v_copy(c, k, size).wait_send()
                return 0

            return lax.fori_loop(1, slab_n, one, 0)

        return step

    lax.fori_loop(0, long_n, sent(CHUNK), 0)
    lax.fori_loop(long_n, chunks, sent(TB), 0)
    own_copy(far_gate).wait_send()
    for i in range(half):
        @pl.when(near_first + i != slab)
        def _():
            own_copy(near_first + i).wait_send()

        for j in range(half):
            @pl.when(jnp.logical_and(at_gate, near_first + j != slab))
            def _():
                far_copy(far_first + i, near_first + j).wait_send()


def on_device(v_slab, t_amp, ab_tile_irrep):
    rows_local, cd = v_slab.shape
    irreps, ij = t_amp.shape[:2]
    amp_n, slab_n = lax.axis_size("amp"), lax.axis_size("slab")
    rows_out = rows_local // slab_n
    ij_all = ij * amp_n
    chunks = rows_out // CHUNK - 1 + CHUNK // TB
    hbm = pl.BlockSpec(memory_space=pltpu.HBM)
    return pl.pallas_call(
        ladder_kernel,
        out_shape=jax.ShapeDtypeStruct((ij_all, rows_out), jnp.bfloat16),
        in_specs=[hbm] * 3,
        out_specs=pl.BlockSpec(memory_space=pltpu.VMEM),
        scratch_shapes=[
            pltpu.SMEM(ab_tile_irrep.shape, jnp.int32),
            pltpu.VMEM((slab_n, ij, irreps, cd), jnp.bfloat16),
            pltpu.VMEM((slab_n, cd // LANES, ij * irreps, LANES), jnp.float32),
            pltpu.VMEM((amp_n, 2, slab_n, ij, cd), jnp.bfloat16),
            pltpu.VMEM((amp_n, 2, slab_n, ij, cd), jnp.bfloat16),
            pltpu.VMEM((ij_all, cd), jnp.float32),
            pltpu.VMEM((2, slab_n, ij_all, cd), jnp.bfloat16),
            pltpu.VMEM((slab_n, rows_out, cd), jnp.bfloat16),
            pltpu.SemaphoreType.DMA((3,)),
            pltpu.SemaphoreType.DMA((slab_n, slab_n)),
            pltpu.SemaphoreType.DMA((slab_n,)),
            pltpu.SemaphoreType.DMA((amp_n,)),
            pltpu.SemaphoreType.DMA((amp_n,)),
            pltpu.SemaphoreType.DMA((chunks, slab_n)),
            pltpu.SemaphoreType.DMA((chunks, slab_n)),
        ],
        compiler_params=pltpu.CompilerParams(
            collective_id=0, has_side_effects=True, vmem_limit_bytes=40 * 1024 * 1024
        ),
        cost_estimate=pl.CostEstimate(
            flops=2 * rows_out * cd * slab_n * ij_all,
            bytes_accessed=2 * (rows_local * cd + rows_out * ij_all),
            transcendentals=0,
        ),
    )(*[pltpu.with_memory_space_constraint(x, pltpu.HBM) for x in (ab_tile_irrep, t_amp.transpose(1, 0, 2), v_slab)]).T


def solution(mesh):
    placed = (P("amp", "slab"), P(None, "amp", "slab"), P())
    return jax.shard_map(
        on_device, mesh=mesh, in_specs=placed, out_specs=P(("amp", "slab"), None), check_vma=False
    )
```
